32 devices in a mesh: tank: 2 (over y), slab: 4 (over z), cross: 2 (over x), sub: 2 (over core).
Axes of the slice: x: 2, y: 2, z: 4, core: 2. Of those that a mesh axis runs over, the one named last changes fastest.
Arguments:
- positions: float32 [3, 64, 64, 128], P(None, ('tank', 'slab'), ('cross', 'sub')), parts along dimension 1, as said below
- velocities: float32 [3, 64, 64, 128], P(None, ('tank', 'slab'), ('cross', 'sub')), parts along dimension 1, may hold values from -6 to 6
- pair_i: int32 [8, 4, 1152], P(('tank', 'slab'), ('cross', 'sub')), parts along dimension 0, may hold values from 0 to 127, as said below
- pair_j: int32 [8, 4, 1152], P(('tank', 'slab'), ('cross', 'sub')), parts along dimension 0, may hold values from 0 to 179, as said below
- pair_count: int32 [8, 4], P(('tank', 'slab'), ('cross', 'sub')), parts along dimension 0, may hold values from 128 to 1152, as said below
- block_fill: int32 [64, 64], P(('tank', 'slab'), ('cross', 'sub')), parts along dimension 0, may hold values from 0 to 128, as said below
- block_body: int32 [64, 64], P(('tank', 'slab'), ('cross', 'sub')), parts along dimension 0, may hold values from 0 to 4
Outputs:
- density: float32 [64, 64, 128], P(('tank', 'slab'), ('cross', 'sub')), parts along dimension 0
- accel: float32 [3, 64, 64, 128], P(None, ('tank', 'slab'), ('cross', 'sub')), parts along dimension 1
- body_force: float32 [3, 8], P(None, 'tank'), parts along dimension 1
The draws below stay inside these ranges and needn't reach their ends.
There are 2 independent parts, one for each index of `tank`. The reference program is written for one: setup_inputs(seed, part) draws one part's arguments, and reference() takes and returns one part's arrays. A program takes and returns all parts, laid end to end along the dimension named above; each array names one. Nothing has to cross between parts.
Inputs may be any that keep to these rules, and one draw needn't show every extreme that they name: `pair_i`: slots 0 to 127 of each row pair local block k with itself (extended block (k // 16 + 1) (18) + k % 16 + 1); the other slots pair each local block once with each of its eight neighbouring extended blocks, in a drawn order, those in which both blocks lie in the tank and have block_fill above 0 coming first. `pair_j`: see pair_i. pair_count is 128 plus the number of neighbour slots whose two blocks both lie in the tank and have block_fill above 0. `block_fill`: a block holds either no particles or 64 to 128. `block_body`: the value 4 marks a free fluid block. `positions`: particles of global block (a, b) have first coordinate in [2.6 a, 2.6 (a + 1)), second in [2.6 b, 2.6 (b + 1)) and third in [0, 18.9).
All inputs are finite; a program needn't handle non-finite values.
Results may differ from the reference program's by a relative error of at most 0.0003.
Values sent between devices are 32-bit elements; how exact they have to be, the bound alone decides.
A program may use at most 64 MiB of HBM per device.

```python
import math
import jax
import jax.numpy as jnp
from jax import lax

BL = 8
BW = 16
NBODY = 4
PMAX = 1152
LX = 32
WY = 64
N_SLAB = 4
N_CROSS = 2
N_SUB = 2


CELL_SIZE = 2.6


WATER_DEPTH = 18.9


def wet_fill(key):
    hull_slabs = max(N_SLAB // 8, 1)
    first_slab = jax.random.randint(jax.random.fold_in(key, 23), (), 1, N_SLAB - hull_slabs)
    levels = jax.random.randint(jax.random.fold_in(key, 29), (N_SLAB,), 3, 10)
    rows = jnp.arange(LX, dtype=jnp.int32)
    hull_rows = (rows >= first_slab * BL - 1) & (rows < (first_slab + hull_slabs) * BL + 1)
    row_level = jnp.where(hull_rows, 10, levels[rows // BL])
    dice = jax.random.randint(jax.random.fold_in(key, 31), (LX, WY), 0, 10)
    wet = dice < row_level[:, None]
    counts = jax.random.randint(jax.random.fold_in(key, 37), (LX, WY), 64, 129)
    counts = counts.at[first_slab * BL, 0].set(128)
    return jnp.where(wet, counts, 0).astype(jnp.int32)


def pair_tables(key):
    local_count = BL * BW
    across = N_CROSS * N_SUB
    device_total = N_SLAB * across
    occupied = jnp.pad((wet_fill(key) > 0).astype(jnp.int32), 1)
    local_ids = jnp.arange(local_count, dtype=jnp.int32)
    block_row = local_ids // BW
    block_column = local_ids % BW
    device_ids = jnp.arange(device_total, dtype=jnp.int32)
    global_row = (device_ids // across)[:, None] * BL + block_row[None, :] + 1
    global_column = (device_ids % across)[:, None] * BW + block_column[None, :] + 1
    own_wet = occupied[global_row, global_column]
    cand_first = []
    cand_second = []
    cand_live = []
    for step_row in (-1, 0, 1):
        for step_column in (-1, 0, 1):
            if step_row != 0 or step_column != 0:
                cand_first.append(local_ids)
                cand_second.append((block_row + 1 + step_row) * (BW + 2) + block_column + 1 + step_column)
                cand_live.append(own_wet * occupied[global_row + step_row, global_column + step_column])
    cand_first = jnp.concatenate(cand_first)
    cand_second = jnp.concatenate(cand_second)
    cand_live = jnp.concatenate(cand_live, axis=1)
    self_second = (block_row + 1) * (BW + 2) + block_column + 1
    device_keys = jax.random.split(jax.random.fold_in(key, 17), device_total)
    orders = jax.vmap(lambda one_key: jax.random.permutation(one_key, 8 * local_count))(device_keys)
    permuted_live = jnp.take_along_axis(cand_live, orders, axis=1)
    ranks = jnp.argsort(1 - permuted_live, axis=1, stable=True)
    final_order = jnp.take_along_axis(orders, ranks, axis=1)
    firsts = jnp.concatenate([jnp.broadcast_to(local_ids, (device_total, local_count)), cand_first[final_order]], axis=1)
    seconds = jnp.concatenate([jnp.broadcast_to(self_second, (device_total, local_count)), cand_second[final_order]], axis=1)
    counts = local_count + jnp.sum(cand_live, axis=1)
    return (firsts.reshape(N_SLAB, across, PMAX).astype(jnp.int32), seconds.reshape(N_SLAB, across, PMAX).astype(jnp.int32), counts.reshape(N_SLAB, across).astype(jnp.int32))


def draw_pair_i(key, part):
    return pair_tables(key)[0]


def draw_pair_j(key, part):
    return pair_tables(key)[1]


def draw_pair_count(key, part):
    return pair_tables(key)[2]


def draw_block_fill(key, part):
    return wet_fill(key)


def draw_positions(key, part):
    spread = jax.random.uniform(jax.random.fold_in(key, 41), (3, LX, WY, 128), dtype=jnp.float32)
    lengthwise = (jnp.arange(LX, dtype=jnp.float32)[:, None, None] + spread[0]) * CELL_SIZE
    crosswise = (jnp.arange(WY, dtype=jnp.float32)[None, :, None] + spread[1]) * CELL_SIZE
    vertical = spread[2] * WATER_DEPTH
    return jnp.stack([lengthwise, crosswise, vertical], axis=0).astype(jnp.float32)


def with_ends(entries, own_key, smallest, high):
    spot = [jax.random.randint(jax.random.fold_in(own_key, axis), (), 0, length) for axis, length in enumerate(entries.shape)]
    main_axis = entries.shape.index(max(entries.shape))
    beside = spot[:main_axis] + [(spot[main_axis] + 1) % entries.shape[main_axis]] + spot[main_axis + 1:]
    return entries.at[tuple(spot)].set(smallest).at[tuple(beside)].set(high)


def level_of(rng, extent, cuts, low, top_value):
    def one(axis_at, blocks):
        draws = jax.random.uniform(jax.random.fold_in(jax.random.fold_in(rng, 6), axis_at), (blocks,), jnp.float32, low / len(cuts), top_value / len(cuts))
        return jnp.repeat(jnp.exp(draws), extent[axis_at] // blocks).reshape((-1,) + (1,) * (len(extent) - axis_at - 1))

    factor_of = one(*cuts[0])
    for cut in cuts[1:]:
        factor_of = factor_of * one(*cut)
    return factor_of


def bell_draw(rng, dims, width, limit, shards=(), kind=jnp.bfloat16):
    values = jax.random.normal(rng, dims, jnp.float32) * width
    if len(shards) > 0:
        values = level_of(rng, dims, shards, -0.22, 0.18) * values
    return jnp.clip(values, min=-limit, max=limit).astype(kind)


def setup_inputs(seed: int = 0, part: int = 0) -> dict:
    key_list = jax.random.split(jax.random.key(seed), 8)
    own_keys = jax.random.split(jax.random.fold_in(key_list[7], part), 8)
    positions = draw_positions(jax.random.fold_in(jax.random.fold_in(key_list[7], part), 71), part)
    velocities = bell_draw(own_keys[1], (3, LX, WY, 128), 1.0, 6.0, ((1, 4), (2, 4)), jnp.float32)
    pair_i = draw_pair_i(jax.random.fold_in(jax.random.fold_in(key_list[7], part), 71), part)
    pair_j = draw_pair_j(jax.random.fold_in(jax.random.fold_in(key_list[7], part), 71), part)
    pair_count = draw_pair_count(jax.random.fold_in(jax.random.fold_in(key_list[7], part), 71), part)
    block_fill = draw_block_fill(jax.random.fold_in(jax.random.fold_in(key_list[7], part), 71), part)
    block_body = with_ends(jax.random.randint(own_keys[6], (LX, WY), 0, NBODY + 1), jax.random.fold_in(own_keys[6], 1), 0, NBODY).astype(jnp.int32)
    return {"positions": positions, "velocities": velocities, "pair_i": pair_i, "pair_j": pair_j, "pair_count": pair_count, "block_fill": block_fill, "block_body": block_body}


SMOOTH = 1.3
KERNEL_NORM = 21.0 / (16.0 * math.pi * SMOOTH ** 3)
SLOPE_NORM = 5.0 * KERNEL_NORM / SMOOTH ** 2
VISCOSITY = 0.2
GRAVITY = 1.0

def pair_shape(first_tiles, second_tiles):
    offsets = first_tiles[:, 0:3, :, None] - second_tiles[:, 0:3, None, :]
    distance = jnp.sqrt(lax.optimization_barrier(jnp.sum(offsets * offsets, axis=1))) / SMOOTH
    remain = jnp.maximum(1.0 - 0.5 * distance, 0.0)
    return (offsets, distance, remain)

def density_terms(first_tiles, second_tiles):
    offsets, distance, remain = pair_shape(first_tiles, second_tiles)
    kernel = KERNEL_NORM * remain ** 4 * (2.0 * distance + 1.0)
    return lax.optimization_barrier(jnp.sum(kernel * second_tiles[:, 3, None, :], axis=2))

def force_terms(first_tiles, second_tiles):
    offsets, distance, remain = pair_shape(first_tiles, second_tiles)
    slope = SLOPE_NORM * remain ** 3 * second_tiles[:, 3, None, :]
    pushed = slope * (first_tiles[:, 7, :, None] + second_tiles[:, 7, None, :])
    push_sum = lax.optimization_barrier(jnp.sum(pushed[:, None] * offsets, axis=3))
    drift = first_tiles[:, 4:7, :, None] - second_tiles[:, 4:7, None, :]
    drag_sum = lax.optimization_barrier(jnp.sum(slope[:, None] * drift, axis=3))
    return push_sum - VISCOSITY * drag_sum

def tile_loop(begin_slot, end_slot, total_slots, group_size, fetch_tiles, kernel, store_values, initial):
    first_group = begin_slot // group_size
    last_group = (end_slot + group_size - 1) // group_size

    def advance(group_index, carried):
        nominal = group_index * group_size
        anchor = jnp.minimum(nominal, total_slots - group_size).astype(jnp.int32)
        slot_ids = anchor + lax.broadcasted_iota(jnp.int32, (group_size,), 0)
        wanted = (slot_ids >= jnp.maximum(begin_slot, nominal)) & (slot_ids < jnp.minimum(end_slot, nominal + group_size))
        first_tiles, second_tiles = fetch_tiles(anchor)
        values = kernel(first_tiles, second_tiles)
        weight = wanted.astype(jnp.float32).reshape((group_size,) + (1,) * (values.ndim - 1))
        return store_values(carried, anchor, values * weight)
    return lax.fori_loop(first_group, last_group, advance, initial)

def table_fetch(table, firsts, seconds, group_size):

    def fetch_tiles(anchor):
        first_ids = lax.dynamic_slice_in_dim(firsts, anchor, group_size)
        second_ids = lax.dynamic_slice_in_dim(seconds, anchor, group_size)
        return (jnp.take(table, first_ids, axis=0), jnp.take(table, second_ids, axis=0))
    return fetch_tiles

def scatter_store(targets, group_size):

    def store_values(carried, anchor, values):
        target_ids = lax.dynamic_slice_in_dim(targets, anchor, group_size)
        return carried.at[target_ids].add(values)
    return store_values

def to_global(per_device, across):
    trailing = per_device.shape[2:]
    shaped = per_device.reshape((N_SLAB, across, BL, BW) + trailing)
    axes_order = (0, 2, 1, 3) + tuple(range(4, 4 + len(trailing)))
    return jnp.transpose(shaped, axes_order).reshape((LX, WY) + trailing)

def reference(positions, velocities, pair_i, pair_j, pair_count, block_fill, block_body):
    local_count = BL * BW
    across = N_CROSS * N_SUB
    devices_part = N_SLAB * across
    extended = (BL + 2) * (BW + 2)
    group_size = min(16, PMAX)
    slot_ids = lax.broadcasted_iota(jnp.int32, (LX, WY, 128), 2)
    masses = (slot_ids < block_fill[:, :, None]).astype(jnp.float32)
    state = jnp.concatenate([jnp.transpose(positions, (1, 2, 0, 3)), masses[:, :, None, :], jnp.transpose(velocities, (1, 2, 0, 3))], axis=2)
    firsts_all = pair_i.reshape(devices_part, PMAX).astype(jnp.int32)
    ext_firsts_all = ((firsts_all // BW + 1) * (BW + 2) + firsts_all % BW + 1).astype(jnp.int32)
    seconds_all = pair_j.reshape(devices_part, PMAX).astype(jnp.int32)
    live_all = pair_count.reshape(devices_part).astype(jnp.int32)
    device_ids = jnp.arange(devices_part).astype(jnp.int32)
    slab_ids = (device_ids // across).astype(jnp.int32)
    cross_ids = (device_ids % across).astype(jnp.int32)

    def blocks_of(padded, slab_id, cross_id):
        anchor_zero = jnp.zeros((), jnp.int32)
        piece = lax.dynamic_slice(padded, (slab_id * BL, cross_id * BW, anchor_zero, anchor_zero), (BL + 2, BW + 2, padded.shape[2], 128))
        return piece.reshape(extended, padded.shape[2], 128)
    padded_state = jnp.pad(state, ((1, 1), (1, 1), (0, 0), (0, 0)))

    def density_part(inputs):
        slab_id, cross_id, firsts, ext_firsts, seconds, live_count = inputs
        table = blocks_of(padded_state, slab_id, cross_id)
        return tile_loop(0, live_count, PMAX, group_size, table_fetch(table, ext_firsts, seconds, group_size), density_terms, scatter_store(firsts, group_size), jnp.zeros((local_count, 128), jnp.float32))
    density_sums = lax.map(density_part, (slab_ids, cross_ids, firsts_all, ext_firsts_all, seconds_all, live_all))
    raw_density = to_global(density_sums, across)
    density = raw_density * masses
    safe_density = jnp.where(masses > 0, raw_density, 1.0)
    pressure_term = masses * (safe_density ** 7 - 1.0) / (safe_density * safe_density)
    force_state = jnp.concatenate([state, pressure_term[:, :, None, :]], axis=2)
    padded_force = jnp.pad(force_state, ((1, 1), (1, 1), (0, 0), (0, 0)))

    def force_part(inputs):
        slab_id, cross_id, firsts, ext_firsts, seconds, live_count = inputs
        table = blocks_of(padded_force, slab_id, cross_id)
        return tile_loop(0, live_count, PMAX, group_size, table_fetch(table, ext_firsts, seconds, group_size), force_terms, scatter_store(firsts, group_size), jnp.zeros((local_count, 3, 128), jnp.float32))
    force_sums = lax.map(force_part, (slab_ids, cross_ids, firsts_all, ext_firsts_all, seconds_all, live_all))
    hydro = to_global(force_sums, across) * masses[:, :, None, :]
    nothing = jnp.zeros_like(masses)
    gravity = jnp.stack([nothing, nothing, GRAVITY * masses], axis=2)
    accel = jnp.transpose(hydro - gravity, (2, 0, 1, 3))
    block_sums = lax.optimization_barrier(jnp.sum(hydro, axis=3))
    owners = (block_body[:, :, None] == lax.broadcasted_iota(jnp.int32, (LX, WY, NBODY), 2)).astype(jnp.float32)
    body_force = jnp.einsum('xyk,xyb->kb', block_sums, owners, precision=lax.Precision.HIGHEST) / math.sqrt(128.0 * LX * WY)
    return (density, accel, body_force)
```

```python
import math

import jax
import jax.numpy as jnp
import numpy as np
from jax import lax
from jax.experimental import pallas as pl
from jax.experimental.pallas import tpu as pltpu
from jax.sharding import PartitionSpec as P

NBODY = 4
SMOOTH = 1.3
CELL = 2.6
KERNEL_NORM = 21.0 / (16.0 * math.pi * SMOOTH**3)
SLOPE_NORM = 5.0 * KERNEL_NORM / SMOOTH**2
VISCOSITY = 0.2
GRAVITY = 1.0
FAR = 64.0
TINY = 1e-12
STEPS = [(da, db) for da in (-1, 0, 1) for db in (-1, 0, 1)]
FEAT = 64
F32, BF16 = jnp.float32, jnp.bfloat16


def shift_tables():
    scale = np.zeros((9, 8, 8, 128), np.float32)
    added = np.zeros((9, 8, 8, 128), np.float32)
    for k, (da, db) in enumerate(STEPS):
        scale[k, 0:6, 0:4] = 1.0
        scale[k, 0:3, 4] = 1.0
        scale[k, 0:3, 7] = -2.0 * da
        scale[k, 6, 4] = scale[k, 6, 7] = scale[k, 7, 4] = -2.0 * db
        for g in (0, 3, 5):
            added[k, g, 5] = 2.0 * da
            added[k, g, 6] = 2.0 * db
        added[k, 7, 7] = da * da + db * db
    return (
        jnp.asarray(scale.reshape(9, FEAT, 128), BF16),
        jnp.asarray(added.reshape(9, FEAT, 128), BF16),
    )


def split3(value):
    high = value.astype(BF16).astype(F32)
    rest = value - high
    middle = rest.astype(BF16).astype(F32)
    return high, middle, rest - middle


def norm_row(block):
    square = block * block
    return square[0:1] + square[1:2] + square[2:3]


def second_features(block):
    mass = block[3:4]
    x, y, z = block[0:1] * mass, block[1:2] * mass, block[2:3] * mass
    norm = jnp.where(mass > 0, norm_row(block), FAR)
    one = jnp.ones_like(mass)
    high, middle, low = split3(jnp.concatenate([x, y, z, norm, one, x, y, one], axis=0))
    rows = jnp.concatenate([high, high, high, middle, middle, low, high, high], axis=0)
    return rows.T.astype(BF16)


def first_features(block):
    x, y, z = block[0:1], block[1:2], block[2:3]
    zero = jnp.zeros_like(x)
    norm = norm_row(block)
    high, middle, low = split3(
        jnp.concatenate([-2.0 * x, -2.0 * y, -2.0 * z, zero, norm, y, zero, x], axis=0)
    )
    row = lax.broadcasted_iota(jnp.int32, (8, 128), 0)
    unit = (row == 3).astype(F32)
    g0, g1, g2 = high + unit, middle, low
    g6 = jnp.concatenate(
        [zero, zero, zero, zero, high[5:6], zero, zero, middle[5:6]], axis=0
    )
    g7 = jnp.concatenate([zero, zero, zero, zero, low[5:6], zero, zero, zero], axis=0)
    return jnp.concatenate([g0, g1, g2, g0, g1, g0, g6, g7], axis=0).astype(BF16)


def closeness(second, base, scale, added):
    first = base * scale + added
    square = jnp.dot(second, first, preferred_element_type=F32)
    square = jnp.maximum(square, TINY)
    return jnp.maximum(1.0 - square * lax.rsqrt(square), 0.0)


def density_kernel(length, width, e_ref, scale_ref, added_ref, a_ref, dens_ref, press_ref):
    frame = width + 2

    def prepare(e, carry):
        a_ref[e] = second_features(e_ref[e])
        return carry

    lax.fori_loop(0, (length + 2) * frame, prepare, 0)

    def local(i, carry):
        row, column = i // width, i % width
        centre = (row + 1) * frame + column + 1
        block = e_ref[centre]
        base = first_features(block)
        total = jnp.zeros((8, 128), F32)
        for k, (da, db) in enumerate(STEPS):
            rest = closeness(
                a_ref[centre + da * frame + db], base, scale_ref[k], added_ref[k]
            )
            twice = rest * rest
            value = twice * twice * (1.25 - rest)
            total = total + jnp.sum(value.reshape(16, 8, 128), axis=0)
        mass = block[3:4]
        raw = (4.0 * KERNEL_NORM) * jnp.sum(total, axis=0, keepdims=True)
        dens_ref[row, pl.ds(column, 1), :] = raw * mass
        safe = jnp.where(mass > 0, raw, 1.0)
        square = safe * safe
        seventh = square * square * square * safe
        press_ref[row, pl.ds(column, 1), :] = mass * (seventh - 1.0) / square
        return carry

    lax.fori_loop(0, length * width, local, 0)


def force_kernel(
    length, width, e_ref, a_ref, p_ref, scale_ref, added_ref, hydro_ref, c_ref
):
    frame = width + 2

    def placed(block, row, column):
        lane = lax.broadcasted_iota(jnp.int32, (1, 128), 1)
        along = jnp.zeros_like(lane) + (row - length // 2)
        across = jnp.zeros_like(lane) + (column - width // 2)
        return (
            block[0:1] + along.astype(F32),
            block[1:2] + across.astype(F32),
            block[2:3],
        )

    def prepare(e, carry):
        row, column = e // frame, e % frame
        block = e_ref[e]
        mass = block[3:4]
        pressure = p_ref[row, pl.ds(column, 1), :]
        spots = placed(block, row - 1, column - 1)
        rows = [mass, pressure] + [spot * mass for spot in spots]
        for d in range(3):
            rows.append(
                mass * (VISCOSITY * block[4 + d : 5 + d] - CELL * pressure * spots[d])
            )
        high, middle, low = split3(jnp.concatenate(rows, axis=0))
        part = jnp.concatenate(
            [high, middle, low, jnp.zeros_like(low)], axis=0
        ).astype(BF16)
        c_ref[e] = jnp.concatenate([part, part], axis=1)
        return carry

    lax.fori_loop(0, (length + 2) * frame, prepare, 0)

    def local(i, carry):
        row, column = i // width, i % width
        centre = (row + 1) * frame + column + 1
        block = e_ref[centre]
        base = first_features(block)
        total = jnp.zeros((32, 128), F32)
        for k, (da, db) in enumerate(STEPS):
            e = centre + da * frame + db
            rest = closeness(a_ref[e], base, scale_ref[k], added_ref[k])
            slope = rest * rest * rest
            high = slope.astype(BF16)
            low = (slope - high.astype(F32)).astype(BF16)
            total = total + jnp.dot(
                c_ref[e],
                jnp.concatenate([high, low], axis=0),
                preferred_element_type=F32,
            )
        sums = total[0:8] + total[8:16] + total[16:24]
        mass = block[3:4]
        pressure = p_ref[row + 1, pl.ds(column + 1, 1), :]
        spots = placed(block, row, column)
        for d in range(3):
            own = CELL * pressure * spots[d] - VISCOSITY * block[4 + d : 5 + d]
            value = (
                own * sums[0:1]
                + CELL * (spots[d] * sums[1:2] - pressure * sums[2 + d : 3 + d])
                + sums[5 + d : 6 + d]
            )
            hydro_ref[d, row, pl.ds(column, 1), :] = SLOPE_NORM * mass * value
        return carry

    lax.fori_loop(0, length * width, local, 0)


def padded(shard, sides, width):
    for axis, dim in sides:
        devices, length = (lax.axis_size(axis), shard.shape[dim])
        up = [(i, (i + 1) % devices) for i in range(devices - 1)]
        down = [(j, i) for i, j in up]
        last = lax.slice_in_dim(shard, length - width, length, axis=dim)
        initial = lax.slice_in_dim(shard, 0, width, axis=dim)
        before = lax.ppermute(last, axis, up)
        after = lax.ppermute(initial, axis, down)
        shard = jnp.concatenate([before, shard, after], axis=dim)
    return shard


def local_frame(values, blocks, axis):
    whole = (26 * blocks + 5) // 10
    left = (5 * whole - 13 * blocks).astype(F32) / 5.0
    shape = [1, 1, 1]
    shape[axis] = -1
    near = values - whole.astype(F32).reshape(shape)
    return (near + left.reshape(shape)) / CELL - 0.5


VMEM = pl.BlockSpec(memory_space=pltpu.VMEM)
PARAMS = pltpu.CompilerParams(vmem_limit_bytes=48 * 1024 * 1024)
SIDES = (("slab", 0), (("cross", "sub"), 1))


def shards(positions, velocities, pair_i, pair_j, pair_count, block_fill, block_body):
    length, width = block_fill.shape
    count = (length + 2) * (width + 2)
    slot_ids = lax.broadcasted_iota(jnp.int32, (length, width, 128), 2)
    masses = (slot_ids < block_fill[:, :, None]).astype(F32)
    rows = lax.axis_index("slab") * length + jnp.arange(length, dtype=jnp.int32)
    columns = lax.axis_index(("cross", "sub")) * width + jnp.arange(width, dtype=jnp.int32)
    x = local_frame(positions[0], rows, 0)
    y = local_frame(positions[1], columns, 1)
    z = (positions[2] - 9.45) / CELL
    state = jnp.stack(
        [x, y, z, masses, velocities[0], velocities[1], velocities[2], masses], axis=2
    )
    table = padded(state, SIDES, 1).reshape(count, 8, 128)
    scale, added = shift_tables()
    features, density, pressure = pl.pallas_call(
        lambda *refs: density_kernel(length, width, *refs),
        out_shape=(
            jax.ShapeDtypeStruct((count, 128, FEAT), BF16),
            jax.ShapeDtypeStruct((length, width, 128), F32),
            jax.ShapeDtypeStruct((length, width, 128), F32),
        ),
        in_specs=[VMEM] * 3,
        out_specs=(VMEM,) * 3,
        compiler_params=PARAMS,
        name="density",
    )(table, scale, added)
    framed_pressure = padded(pressure, SIDES, 1)
    hydro = pl.pallas_call(
        lambda *refs: force_kernel(length, width, *refs),
        out_shape=jax.ShapeDtypeStruct((3, length, width, 128), F32),
        in_specs=[VMEM] * 5,
        out_specs=VMEM,
        scratch_shapes=[pltpu.VMEM((count, 32, 256), BF16)],
        compiler_params=PARAMS,
        name="force",
    )(table, features, framed_pressure, scale, added)
    down = jnp.array([0.0, 0.0, GRAVITY], F32)[:, None, None, None]
    accel = hydro - down * masses[None]
    block_sums = jnp.sum(hydro, axis=3)
    bodies = lax.broadcasted_iota(jnp.int32, (NBODY, length, width), 0)
    owned = (block_body[None] == bodies).astype(F32)
    partial_force = jnp.sum(block_sums[:, None] * owned[None], axis=(2, 3))
    totals = lax.psum(partial_force, ("slab", "cross", "sub"))
    slot_total = (
        128
        * length
        * lax.axis_size("slab")
        * width
        * lax.axis_size("cross")
        * lax.axis_size("sub")
    )
    return (density, accel, totals / math.sqrt(slot_total))


def solution(mesh):
    placed = (
        P(None, ("tank", "slab"), ("cross", "sub"), None),
        P(None, ("tank", "slab"), ("cross", "sub"), None),
        P(("tank", "slab"), ("cross", "sub"), None),
        P(("tank", "slab"), ("cross", "sub"), None),
        P(("tank", "slab"), ("cross", "sub")),
        P(("tank", "slab"), ("cross", "sub")),
        P(("tank", "slab"), ("cross", "sub")),
    )
    return jax.shard_map(
        shards,
        mesh=mesh,
        in_specs=placed,
        out_specs=(
            P(("tank", "slab"), ("cross", "sub"), None),
            P(None, ("tank", "slab"), ("cross", "sub"), None),
            P(None, "tank"),
        ),
        check_vma=False,
    )
```

```python
import math

import jax
import jax.numpy as jnp
import numpy as np
from jax import lax
from jax.experimental import pallas as pl
from jax.experimental.pallas import tpu as pltpu
from jax.sharding import PartitionSpec as P

NBODY = 4
SMOOTH = 1.3
CELL = 2.6
KERNEL_NORM = 21.0 / (16.0 * math.pi * SMOOTH**3)
SLOPE_NORM = 5.0 * KERNEL_NORM / SMOOTH**2
VISCOSITY = 0.2
GRAVITY = 1.0
FAR = 64.0
TINY = 1e-12
STEPS = [(da, db) for da in (-1, 0, 1) for db in (-1, 0, 1)]
FEAT = 64
F32, BF16 = jnp.float32, jnp.bfloat16


def shift_tables():
    scale = np.zeros((9, 8, 8, 128), np.float32)
    added = np.zeros((9, 8, 8, 128), np.float32)
    for k, (da, db) in enumerate(STEPS):
        scale[k, 0:6, 0:4] = 1.0
        scale[k, 0:3, 4] = 1.0
        scale[k, 0:3, 7] = -2.0 * da
        scale[k, 6, 4] = scale[k, 6, 7] = scale[k, 7, 4] = -2.0 * db
        for g in (0, 3, 5):
            added[k, g, 5] = 2.0 * da
            added[k, g, 6] = 2.0 * db
        added[k, 7, 7] = da * da + db * db
    return (
        jnp.asarray(scale.reshape(9, FEAT, 128), BF16),
        jnp.asarray(added.reshape(9, FEAT, 128), BF16),
    )


def split3(value):
    high = value.astype(BF16).astype(F32)
    rest = value - high
    middle = rest.astype(BF16).astype(F32)
    return high, middle, rest - middle


def norm_row(block):
    square = block * block
    return square[0:1] + square[1:2] + square[2:3]


def second_features(block):
    mass = block[3:4]
    x, y, z = block[0:1] * mass, block[1:2] * mass, block[2:3] * mass
    norm = jnp.where(mass > 0, norm_row(block), FAR)
    one = jnp.ones_like(mass)
    high, middle, low = split3(jnp.concatenate([x, y, z, norm, one, x, y, one], axis=0))
    rows = jnp.concatenate([high, high, high, middle, middle, low, high, high], axis=0)
    return rows.T.astype(BF16)


def first_features(block):
    x, y, z = block[0:1], block[1:2], block[2:3]
    zero = jnp.zeros_like(x)
    norm = norm_row(block)
    high, middle, low = split3(
        jnp.concatenate([-2.0 * x, -2.0 * y, -2.0 * z, zero, norm, y, zero, x], axis=0)
    )
    row = lax.broadcasted_iota(jnp.int32, (8, 128), 0)
    unit = (row == 3).astype(F32)
    g0, g1, g2 = high + unit, middle, low
    g6 = jnp.concatenate(
        [zero, zero, zero, zero, high[5:6], zero, zero, middle[5:6]], axis=0
    )
    g7 = jnp.concatenate([zero, zero, zero, zero, low[5:6], zero, zero, zero], axis=0)
    return jnp.concatenate([g0, g1, g2, g0, g1, g0, g6, g7], axis=0).astype(BF16)


def group_of(count):
    return next(n for n in (6, 5, 4, 3, 2, 1) if count % n == 0)


def pipelined(count, dots, process, first_buffer, second_buffer):
    dots(0, first_buffer)

    def step(pair, carry):
        dots(2 * pair + 1, second_buffer)
        process(2 * pair, first_buffer)
        dots(jnp.minimum(2 * pair + 2, count - 1), first_buffer)
        process(2 * pair + 1, second_buffer)
        return carry

    lax.fori_loop(0, count // 2, step, 0)


def square_dots(width, e_ref, a_ref, scale_ref, added_ref):
    frame = width + 2

    def dots(i, buffer):
        centre = (i // width + 1) * frame + i % width + 1
        base = first_features(e_ref[centre])
        for k, (da, db) in enumerate(STEPS):
            buffer[k] = jnp.dot(
                a_ref[centre + da * frame + db],
                base * scale_ref[k] + added_ref[k],
                preferred_element_type=F32,
            )

    return dots


def closeness(square):
    square = jnp.maximum(square, TINY)
    return jnp.maximum(1.0 - square * lax.rsqrt(square), 0.0)


def density_kernel(
    length, width, e_ref, scale_ref, added_ref, a_ref, dens_ref, table_ref, s0, s1
):
    frame = width + 2
    count = (length + 2) * frame
    group = group_of(count)

    def prepare(step, carry):
        made = [second_features(e_ref[step * group + n]) for n in range(group)]
        for n in range(group):
            a_ref[step * group + n] = made[n]
        return carry

    lax.fori_loop(0, count // group, prepare, 0)

    def process(i, buffer):
        row, column = i // width, i % width
        block = e_ref[(row + 1) * frame + column + 1]
        total = jnp.zeros((8, 128), F32)
        for k in range(9):
            rest = closeness(buffer[k])
            twice = rest * rest
            value = twice * twice * (1.25 - rest)
            total = total + jnp.sum(value.reshape(16, 8, 128), axis=0)
        mass = block[3:4]
        raw = (4.0 * KERNEL_NORM) * jnp.sum(total, axis=0, keepdims=True)
        dens_ref[row, pl.ds(column, 1), :] = raw * mass
        safe = jnp.where(mass > 0, raw, 1.0)
        square = safe * safe
        seventh = square * square * square * safe
        pressure = mass * (seventh - 1.0) / square
        place = lax.broadcasted_iota(jnp.int32, (8, 128), 0)
        table_ref[row, column] = jnp.where(place == 7, pressure, block)

    dots = square_dots(width, e_ref, a_ref, scale_ref, added_ref)
    pipelined(length * width, dots, process, s0, s1)


def force_kernel(
    length,
    width,
    body_ref,
    e_ref,
    a_ref,
    scale_ref,
    added_ref,
    accel_ref,
    sum_ref,
    c_ref,
    s0,
    s1,
):
    frame = width + 2
    count = (length + 2) * frame
    group = group_of(count)
    sum_ref[...] = jnp.zeros_like(sum_ref)

    def placed(block, row, column):
        lane = lax.broadcasted_iota(jnp.int32, (1, 128), 1)
        along = jnp.zeros_like(lane) + (row - length // 2)
        across = jnp.zeros_like(lane) + (column - width // 2)
        return (
            block[0:1] + along.astype(F32),
            block[1:2] + across.astype(F32),
            block[2:3],
        )

    def weights(e):
        block = e_ref[e]
        mass, pressure = block[3:4], block[7:8]
        spots = placed(block, e // frame - 1, e % frame - 1)
        rows = [mass, pressure] + [spot * mass for spot in spots]
        for d in range(3):
            rows.append(
                mass * (VISCOSITY * block[4 + d : 5 + d] - CELL * pressure * spots[d])
            )
        high, middle, low = split3(jnp.concatenate(rows, axis=0))
        part = jnp.concatenate(
            [high, middle, low, jnp.zeros_like(low)], axis=0
        ).astype(BF16)
        return jnp.concatenate([part, part], axis=1)

    def prepare(step, carry):
        made = [weights(step * group + n) for n in range(group)]
        for n in range(group):
            c_ref[step * group + n] = made[n]
        return carry

    lax.fori_loop(0, count // group, prepare, 0)

    def process(i, buffer):
        row, column = i // width, i % width
        centre = (row + 1) * frame + column + 1
        block = e_ref[centre]
        total = jnp.zeros((32, 128), F32)
        for k, (da, db) in enumerate(STEPS):
            rest = closeness(buffer[k])
            slope = rest * rest * rest
            high = slope.astype(BF16)
            low = (slope - high.astype(F32)).astype(BF16)
            total = total + jnp.dot(
                c_ref[centre + da * frame + db],
                jnp.concatenate([high, low], axis=0),
                preferred_element_type=F32,
            )
        sums = total[0:8] + total[8:16] + total[16:24]
        mass, pressure = block[3:4], block[7:8]
        spots = placed(block, row, column)
        rows = []
        for d in range(3):
            own = CELL * pressure * spots[d] - VISCOSITY * block[4 + d : 5 + d]
            value = (
                own * sums[0:1]
                + CELL * (spots[d] * sums[1:2] - pressure * sums[2 + d : 3 + d])
                + sums[5 + d : 6 + d]
            )
            hydro = SLOPE_NORM * mass * value
            rows.append(hydro)
            shown = hydro - GRAVITY * mass if d == 2 else hydro
            accel_ref[d, row, pl.ds(column, 1), :] = shown
        owner = body_ref[row, column]
        rows += [jnp.zeros((5, 128), F32)]
        sum_ref[owner] = sum_ref[owner] + jnp.concatenate(rows, axis=0)

    dots = square_dots(width, e_ref, a_ref, scale_ref, added_ref)
    pipelined(length * width, dots, process, s0, s1)


def sides():
    subs = lax.axis_size("sub")
    slab = lax.axis_index("slab")
    across = lax.axis_index("cross") * subs + lax.axis_index("sub")
    return slab, lax.axis_size("slab"), across, lax.axis_size("cross") * subs


def neighbour(slab, across):
    subs = lax.axis_size("sub")
    return {"slab": slab, "cross": across // subs, "sub": across % subs}


def halo(length, width, out_ref, send_sems, recv_sems):
    slab, slabs, across, acrosses = sides()
    away = [(da, db) for da, db in STEPS if (da, db) != (0, 0)]

    def inside(da, db):
        row, column = slab + da, across + db
        return (row >= 0) & (row < slabs) & (column >= 0) & (column < acrosses)

    barrier = pltpu.get_barrier_semaphore()
    near = jnp.int32(0)
    for da, db in away:

        @pl.when(inside(da, db))
        def _():
            pl.semaphore_signal(
                barrier, inc=1, device_id=neighbour(slab + da, across + db)
            )

        near = near + inside(da, db).astype(jnp.int32)
    pl.semaphore_wait(barrier, near)

    def edge(step, size):
        mine = {-1: (1, 1), 0: (1, size), 1: (size, 1)}[step]
        theirs = {-1: (size + 1, 1), 0: (1, size), 1: (0, 1)}[step]
        return pl.ds(*mine), pl.ds(*theirs)

    def copy(n, da, db, to_row, to_column):
        (from_a, to_a), (from_b, to_b) = edge(da, length), edge(db, width)
        return pltpu.make_async_remote_copy(
            src_ref=out_ref.at[from_a, from_b],
            dst_ref=out_ref.at[to_a, to_b],
            send_sem=send_sems.at[n],
            recv_sem=recv_sems.at[n],
            device_id=neighbour(to_row, to_column),
        )

    for n, (da, db) in enumerate(away):

        @pl.when(inside(da, db))
        def _():
            copy(n, da, db, slab + da, across + db).start()

    for n, (da, db) in enumerate(away):

        @pl.when(inside(da, db))
        def _():
            copy(n, da, db, slab + da, across + db).wait_send()

        @pl.when(inside(-da, -db))
        def _():
            copy(n, da, db, slab - da, across - db).wait_recv()


def clear_frame(length, width, out_ref):
    out_ref[0] = jnp.zeros(out_ref.shape[1:], F32)
    out_ref[length + 1] = jnp.zeros(out_ref.shape[1:], F32)

    def clear(row, carry):
        out_ref[row, 0] = jnp.zeros((8, 128), F32)
        out_ref[row, width + 1] = jnp.zeros((8, 128), F32)
        return carry

    lax.fori_loop(1, length + 1, clear, 0)


def pack_kernel(length, width, x_ref, v_ref, mass_ref, out_ref, send_sems, recv_sems):
    slab, _, across, _ = sides()
    clear_frame(length, width, out_ref)

    def frame_of(block):
        whole = (26 * block + 5) // 10
        return whole.astype(F32), (5 * whole - 13 * block).astype(F32) / 5.0

    def pack(row, carry):
        start_a, left_a = frame_of(slab * length + row)
        for column in range(width):
            start_b, left_b = frame_of(across * width + column)
            x = [x_ref[d, row, column : column + 1, :] for d in range(3)]
            v = [v_ref[d, row, column : column + 1, :] for d in range(3)]
            mass = mass_ref[row, column : column + 1, :]
            rows = [
                ((x[0] - start_a) + left_a) / CELL - 0.5,
                ((x[1] - start_b) + left_b) / CELL - 0.5,
                (x[2] - 9.45) / CELL,
                mass,
            ]
            out_ref[row + 1, column + 1] = jnp.concatenate(rows + v + [mass], axis=0)
        return carry

    lax.fori_loop(0, length, pack, 0)
    halo(length, width, out_ref, send_sems, recv_sems)


def frame_kernel(length, width, table_ref, out_ref, send_sems, recv_sems):
    clear_frame(length, width, out_ref)

    def place(row, carry):
        out_ref[row + 1, 1 : width + 1] = table_ref[row]
        return carry

    lax.fori_loop(0, length, place, 0)
    halo(length, width, out_ref, send_sems, recv_sems)


def total_kernel(part_ref, out_ref, held, near, far, send_sems, recv_sems):
    slab, slabs, across, acrosses = sides()
    barrier = pltpu.get_barrier_semaphore()
    beside = lambda n: neighbour(slab, lax.rem(across + n, acrosses))
    along = lambda n: neighbour(lax.rem(slab + n, slabs), across)
    for n in range(1, acrosses):
        pl.semaphore_signal(barrier, inc=1, device_id=beside(n))
    for n in range(1, slabs):
        pl.semaphore_signal(barrier, inc=1, device_id=along(n))
    pl.semaphore_wait(barrier, acrosses + slabs - 2)

    def swap(source, landing, size, peer, first):
        copies = []
        for n in range(1, size):
            copies.append(
                pltpu.make_async_remote_copy(
                    src_ref=source,
                    dst_ref=landing.at[n - 1],
                    send_sem=send_sems.at[first + n - 1],
                    recv_sem=recv_sems.at[first + n - 1],
                    device_id=peer(n),
                )
            )
            copies[-1].start()
        value = source[...]
        for n, copy in enumerate(copies):
            copy.wait()
            value = value + landing[n]
        return value

    held[...] = swap(part_ref, near, acrosses, beside, 0)
    value = swap(held, far, slabs, along, acrosses - 1)
    out_ref[...] = jnp.broadcast_to(jnp.sum(value, axis=2, keepdims=True), value.shape)


VMEM = pl.BlockSpec(memory_space=pltpu.VMEM)
SMEM = pl.BlockSpec(memory_space=pltpu.SMEM)
LIMIT = 48 * 1024 * 1024
PARAMS = pltpu.CompilerParams(vmem_limit_bytes=LIMIT)


def remote(number):
    return pltpu.CompilerParams(
        vmem_limit_bytes=LIMIT, collective_id=number, has_side_effects=True
    )


def shards(positions, velocities, pair_i, pair_j, pair_count, block_fill, block_body):
    length, width = block_fill.shape
    count = (length + 2) * (width + 2)
    slot_ids = lax.broadcasted_iota(jnp.int32, (length, width, 128), 2)
    masses = (slot_ids < block_fill[:, :, None]).astype(F32)
    framed = jax.ShapeDtypeStruct((length + 2, width + 2, 8, 128), F32)
    eight = [pltpu.SemaphoreType.DMA((8,))] * 2
    ahead = [pltpu.VMEM((9, 128, 128), F32)] * 2
    table = pl.pallas_call(
        lambda *refs: pack_kernel(length, width, *refs),
        out_shape=framed,
        in_specs=[VMEM] * 3,
        out_specs=VMEM,
        scratch_shapes=eight,
        compiler_params=remote(0),
        name="pack",
    )(positions, velocities, masses)
    scale, added = shift_tables()
    features, density, pressed = pl.pallas_call(
        lambda *refs: density_kernel(length, width, *refs),
        out_shape=(
            jax.ShapeDtypeStruct((count, 128, FEAT), BF16),
            jax.ShapeDtypeStruct((length, width, 128), F32),
            jax.ShapeDtypeStruct((length, width, 8, 128), F32),
        ),
        in_specs=[VMEM] * 3,
        out_specs=(VMEM,) * 3,
        scratch_shapes=ahead,
        compiler_params=PARAMS,
        name="density",
    )(table.reshape(count, 8, 128), scale, added)
    table = pl.pallas_call(
        lambda *refs: frame_kernel(length, width, *refs),
        out_shape=framed,
        in_specs=[VMEM],
        out_specs=VMEM,
        scratch_shapes=eight,
        compiler_params=remote(1),
        name="frame",
    )(pressed)
    accel, partial_force = pl.pallas_call(
        lambda *refs: force_kernel(length, width, *refs),
        out_shape=(
            jax.ShapeDtypeStruct((3, length, width, 128), F32),
            jax.ShapeDtypeStruct((NBODY + 1, 8, 128), F32),
        ),
        in_specs=[SMEM] + [VMEM] * 4,
        out_specs=(VMEM, VMEM),
        scratch_shapes=[pltpu.VMEM((count, 32, 256), BF16)] + ahead,
        compiler_params=PARAMS,
        name="force",
    )(block_body, table.reshape(count, 8, 128), features, scale, added)
    slabs = lax.axis_size("slab")
    acrosses = lax.axis_size("cross") * lax.axis_size("sub")
    one = partial_force.shape
    totals = pl.pallas_call(
        total_kernel,
        out_shape=jax.ShapeDtypeStruct(one, F32),
        in_specs=[VMEM],
        out_specs=VMEM,
        scratch_shapes=[
            pltpu.VMEM(one, F32),
            pltpu.VMEM((acrosses - 1,) + one, F32),
            pltpu.VMEM((slabs - 1,) + one, F32),
        ]
        + [pltpu.SemaphoreType.DMA((acrosses + slabs - 2,))] * 2,
        compiler_params=remote(2),
        name="total",
    )(partial_force)
    slot_total = 128 * length * slabs * width * acrosses
    body_force = totals[:NBODY, :3, 0].T / math.sqrt(slot_total)
    return (density, accel, body_force)


def solution(mesh):
    placed = (
        P(None, ("tank", "slab"), ("cross", "sub"), None),
        P(None, ("tank", "slab"), ("cross", "sub"), None),
        P(("tank", "slab"), ("cross", "sub"), None),
        P(("tank", "slab"), ("cross", "sub"), None),
        P(("tank", "slab"), ("cross", "sub")),
        P(("tank", "slab"), ("cross", "sub")),
        P(("tank", "slab"), ("cross", "sub")),
    )
    return jax.shard_map(
        shards,
        mesh=mesh,
        in_specs=placed,
        out_specs=(
            P(("tank", "slab"), ("cross", "sub"), None),
            P(None, ("tank", "slab"), ("cross", "sub"), None),
            P(None, "tank"),
        ),
        check_vma=False,
    )
```

```python
import math

import jax
import jax.numpy as jnp
from jax import lax
from jax.experimental import pallas as pl
from jax.experimental.pallas import tpu as pltpu
from jax.sharding import PartitionSpec as P

NBODY = 4
SMOOTH = 1.3
CELL = 2.6
KERNEL_NORM = 21.0 / (16.0 * math.pi * SMOOTH**3)
SLOPE_NORM = 5.0 * KERNEL_NORM / SMOOTH**2
VISCOSITY = 0.2
GRAVITY = 1.0
FAR = 1024.0
TINY = 1e-12
STEPS = [(da, db) for da in (-1, 0, 1) for db in (-1, 0, 1)]
FEAT = 48
F32, BF16 = jnp.float32, jnp.bfloat16


def placed(block, row, column, length, width):
    lane = lax.broadcasted_iota(jnp.int32, (1, 128), 1)
    along = (jnp.zeros_like(lane) + row).astype(F32) - 0.5 * (length - 1)
    across = (jnp.zeros_like(lane) + column).astype(F32) - 0.5 * (width - 1)
    return block[0:1] + along, block[1:2] + across, block[2:3]


def split3(value):
    high = value.astype(BF16).astype(F32)
    rest = value - high
    middle = rest.astype(BF16).astype(F32)
    return high, middle, rest - middle


def second_features(spots, mass):
    x, y, z = [spot * mass for spot in spots]
    norm = jnp.where(mass > 0, x * x + y * y + z * z, FAR)
    one, zero = jnp.ones_like(mass), jnp.zeros_like(mass)
    high, middle, low = split3(
        jnp.concatenate([x, y, z, norm, one, zero, zero, zero], axis=0)
    )
    rows = jnp.concatenate([high, high, high, middle, middle, low], axis=0)
    return jnp.concatenate([rows, jnp.zeros((16, 128), F32)], axis=0).T[:, :FEAT].astype(BF16)


def first_features(spots):
    x, y, z = spots
    zero = jnp.zeros_like(x)
    norm = x * x + y * y + z * z
    high, middle, low = split3(
        jnp.concatenate(
            [-2.0 * x, -2.0 * y, -2.0 * z, zero, norm, zero, zero, zero], axis=0
        )
    )
    unit = (lax.broadcasted_iota(jnp.int32, (8, 128), 0) == 3).astype(F32)
    high = high + unit
    return jnp.concatenate([high, middle, low, high, middle, high], axis=0).astype(BF16)


def group_of(count):
    return next(n for n in (6, 5, 4, 3, 2, 1) if count % n == 0)


def pipelined(count, dots, process, first_buffer, second_buffer):
    dots(0, first_buffer)

    def step(pair, carry):
        dots(2 * pair + 1, second_buffer)
        process(2 * pair, first_buffer)
        dots(jnp.minimum(2 * pair + 2, count - 1), first_buffer)
        process(2 * pair + 1, second_buffer)
        return carry

    lax.fori_loop(0, count // 2, step, 0)


def square_dots(length, width, e_ref, a_ref):
    frame = width + 2

    def dots(i, buffer):
        row, column = i // width, i % width
        centre = (row + 1) * frame + column + 1
        first = first_features(placed(e_ref[centre], row, column, length, width))
        for k, (da, db) in enumerate(STEPS):
            buffer[k] = jnp.dot(
                a_ref[centre + da * frame + db], first, preferred_element_type=F32
            )

    return dots


def closeness(square):
    square = jnp.maximum(square, TINY)
    return jnp.maximum(1.0 - square * lax.rsqrt(square), 0.0)


def density_kernel(
    length, width, e_ref, a_ref, dens_ref, table_ref, s0, s1
):
    frame = width + 2
    count = (length + 2) * frame
    group = group_of(count)

    def prepare(step, carry):
        made = []
        for n in range(group):
            e = step * group + n
            block = e_ref[e]
            spots = placed(block, e // frame - 1, e % frame - 1, length, width)
            made.append(second_features(spots, block[3:4]))
        for n in range(group):
            a_ref[step * group + n] = made[n]
        return carry

    lax.fori_loop(0, count // group, prepare, 0)

    def process(i, buffer):
        row, column = i // width, i % width
        block = e_ref[(row + 1) * frame + column + 1]
        total = jnp.zeros((8, 128), F32)
        for k in range(9):
            rest = closeness(buffer[k])
            twice = rest * rest
            value = twice * twice * (1.25 - rest)
            total = total + jnp.sum(value.reshape(16, 8, 128), axis=0)
        mass = block[3:4]
        raw = (4.0 * KERNEL_NORM) * jnp.sum(total, axis=0, keepdims=True)
        dens_ref[row, pl.ds(column, 1), :] = raw * mass
        safe = jnp.where(mass > 0, raw, 1.0)
        square = safe * safe
        seventh = square * square * square * safe
        pressure = mass * (seventh - 1.0) / square
        place = lax.broadcasted_iota(jnp.int32, (8, 128), 0)
        table_ref[row, column] = jnp.where(place == 7, pressure, block)

    dots = square_dots(length, width, e_ref, a_ref)
    pipelined(length * width, dots, process, s0, s1)


def force_kernel(
    length,
    width,
    body_ref,
    e_ref,
    a_ref,
    accel_ref,
    sum_ref,
    c_ref,
    s0,
    s1,
):
    frame = width + 2
    count = (length + 2) * frame
    group = group_of(count)
    sum_ref[...] = jnp.zeros_like(sum_ref)

    def weights(e):
        block = e_ref[e]
        mass, pressure = block[3:4], block[7:8]
        spots = placed(block, e // frame - 1, e % frame - 1, length, width)
        rows = [mass, pressure] + [spot * mass for spot in spots]
        for d in range(3):
            rows.append(
                mass * (VISCOSITY * block[4 + d : 5 + d] - CELL * pressure * spots[d])
            )
        high, middle, low = split3(jnp.concatenate(rows, axis=0))
        part = jnp.concatenate(
            [high, middle, low, jnp.zeros_like(low)], axis=0
        ).astype(BF16)
        return jnp.concatenate([part, part], axis=1)

    def prepare(step, carry):
        made = [weights(step * group + n) for n in range(group)]
        for n in range(group):
            c_ref[step * group + n] = made[n]
        return carry

    lax.fori_loop(0, count // group, prepare, 0)

    def process(i, buffer):
        row, column = i // width, i % width
        centre = (row + 1) * frame + column + 1
        block = e_ref[centre]
        total = jnp.zeros((32, 128), F32)

        def halves(k):
            rest = closeness(buffer[k])
            slope = rest * rest * rest
            high = slope.astype(BF16)
            low = (slope - high.astype(F32)).astype(BF16)
            return jnp.concatenate([high, low], axis=0)

        def features(k):
            da, db = STEPS[k]
            return c_ref[centre + da * frame + db]

        for k in range(0, 8, 2):
            both = jnp.dot(
                jnp.concatenate([features(k), features(k + 1)], axis=0),
                jnp.concatenate([halves(k), halves(k + 1)], axis=1),
                preferred_element_type=F32,
            )
            total = total + both[0:32, 0:128] + both[32:64, 128:256]
        total = total + jnp.dot(features(8), halves(8), preferred_element_type=F32)
        sums = total[0:8] + total[8:16] + total[16:24]
        mass, pressure = block[3:4], block[7:8]
        spots = placed(block, row, column, length, width)
        rows = []
        for d in range(3):
            own = CELL * pressure * spots[d] - VISCOSITY * block[4 + d : 5 + d]
            value = (
                own * sums[0:1]
                + CELL * (spots[d] * sums[1:2] - pressure * sums[2 + d : 3 + d])
                + sums[5 + d : 6 + d]
            )
            hydro = SLOPE_NORM * mass * value
            rows.append(hydro)
            shown = hydro - GRAVITY * mass if d == 2 else hydro
            accel_ref[d, row, pl.ds(column, 1), :] = shown
        owner = body_ref[row, column]
        rows += [jnp.zeros((5, 128), F32)]
        sum_ref[owner] = sum_ref[owner] + jnp.concatenate(rows, axis=0)

    dots = square_dots(length, width, e_ref, a_ref)
    pipelined(length * width, dots, process, s0, s1)


def sides():
    subs = lax.axis_size("sub")
    slab = lax.axis_index("slab")
    across = lax.axis_index("cross") * subs + lax.axis_index("sub")
    return slab, lax.axis_size("slab"), across, lax.axis_size("cross") * subs


def neighbour(slab, across):
    subs = lax.axis_size("sub")
    return {"slab": slab, "cross": across // subs, "sub": across % subs}


def halo(length, width, out_ref, send_sems, recv_sems):
    slab, slabs, across, acrosses = sides()
    away = [(da, db) for da, db in STEPS if (da, db) != (0, 0)]

    def inside(da, db):
        row, column = slab + da, across + db
        return (row >= 0) & (row < slabs) & (column >= 0) & (column < acrosses)

    barrier = pltpu.get_barrier_semaphore()
    near = jnp.int32(0)
    for da, db in away:

        @pl.when(inside(da, db))
        def _():
            pl.semaphore_signal(
                barrier, inc=1, device_id=neighbour(slab + da, across + db)
            )

        near = near + inside(da, db).astype(jnp.int32)
    pl.semaphore_wait(barrier, near)

    def edge(step, size):
        mine = {-1: (1, 1), 0: (1, size), 1: (size, 1)}[step]
        theirs = {-1: (size + 1, 1), 0: (1, size), 1: (0, 1)}[step]
        return pl.ds(*mine), pl.ds(*theirs)

    def copy(n, da, db, to_row, to_column):
        (from_a, to_a), (from_b, to_b) = edge(da, length), edge(db, width)
        return pltpu.make_async_remote_copy(
            src_ref=out_ref.at[from_a, from_b],
            dst_ref=out_ref.at[to_a, to_b],
            send_sem=send_sems.at[n],
            recv_sem=recv_sems.at[n],
            device_id=neighbour(to_row, to_column),
        )

    for n, (da, db) in enumerate(away):

        @pl.when(inside(da, db))
        def _():
            copy(n, da, db, slab + da, across + db).start()

    for n, (da, db) in enumerate(away):

        @pl.when(inside(da, db))
        def _():
            copy(n, da, db, slab + da, across + db).wait_send()

        @pl.when(inside(-da, -db))
        def _():
            copy(n, da, db, slab - da, across - db).wait_recv()


def clear_frame(length, width, out_ref):
    out_ref[0] = jnp.zeros(out_ref.shape[1:], F32)
    out_ref[length + 1] = jnp.zeros(out_ref.shape[1:], F32)

    def clear(row, carry):
        out_ref[row, 0] = jnp.zeros((8, 128), F32)
        out_ref[row, width + 1] = jnp.zeros((8, 128), F32)
        return carry

    lax.fori_loop(1, length + 1, clear, 0)


def pack_kernel(length, width, x_ref, v_ref, fill_ref, out_ref, send_sems, recv_sems):
    slab, _, across, _ = sides()
    slot = lax.broadcasted_iota(jnp.int32, (1, 128), 1)
    clear_frame(length, width, out_ref)

    def frame_of(block):
        whole = (26 * block + 5) // 10
        return whole.astype(F32), (5 * whole - 13 * block).astype(F32) / 5.0

    def pack(row, carry):
        start_a, left_a = frame_of(slab * length + row)
        for column in range(width):
            start_b, left_b = frame_of(across * width + column)
            x = [x_ref[d, row, column : column + 1, :] for d in range(3)]
            v = [v_ref[d, row, column : column + 1, :] for d in range(3)]
            mass = (slot < fill_ref[row, column]).astype(F32)
            rows = [
                ((x[0] - start_a) + left_a) / CELL - 0.5,
                ((x[1] - start_b) + left_b) / CELL - 0.5,
                (x[2] - 9.45) / CELL,
                mass,
            ]
            out_ref[row + 1, column + 1] = jnp.concatenate(rows + v + [mass], axis=0)
        return carry

    lax.fori_loop(0, length, pack, 0)
    halo(length, width, out_ref, send_sems, recv_sems)


def frame_kernel(length, width, table_ref, out_ref, send_sems, recv_sems):
    clear_frame(length, width, out_ref)

    def place(row, carry):
        out_ref[row + 1, 1 : width + 1] = table_ref[row]
        return carry

    lax.fori_loop(0, length, place, 0)
    halo(length, width, out_ref, send_sems, recv_sems)


def total_kernel(part_ref, out_ref, held, near, far, send_sems, recv_sems):
    slab, slabs, across, acrosses = sides()
    barrier = pltpu.get_barrier_semaphore()
    beside = lambda n: neighbour(slab, lax.rem(across + n, acrosses))
    along = lambda n: neighbour(lax.rem(slab + n, slabs), across)
    for n in range(1, acrosses):
        pl.semaphore_signal(barrier, inc=1, device_id=beside(n))
    for n in range(1, slabs):
        pl.semaphore_signal(barrier, inc=1, device_id=along(n))
    pl.semaphore_wait(barrier, acrosses + slabs - 2)

    def swap(source, landing, size, peer, first):
        copies = []
        for n in range(1, size):
            copies.append(
                pltpu.make_async_remote_copy(
                    src_ref=source,
                    dst_ref=landing.at[n - 1],
                    send_sem=send_sems.at[first + n - 1],
                    recv_sem=recv_sems.at[first + n - 1],
                    device_id=peer(n),
                )
            )
            copies[-1].start()
        value = source[...]
        for n, copy in enumerate(copies):
            copy.wait()
            value = value + landing[n]
        return value

    held[...] = swap(part_ref, near, acrosses, beside, 0)
    value = swap(held, far, slabs, along, acrosses - 1)
    out_ref[...] = jnp.broadcast_to(jnp.sum(value, axis=2, keepdims=True), value.shape)


VMEM = pl.BlockSpec(memory_space=pltpu.VMEM)
SMEM = pl.BlockSpec(memory_space=pltpu.SMEM)
LIMIT = 48 * 1024 * 1024
PARAMS = pltpu.CompilerParams(vmem_limit_bytes=LIMIT)


def remote(number):
    return pltpu.CompilerParams(
        vmem_limit_bytes=LIMIT, collective_id=number, has_side_effects=True
    )


def shards(positions, velocities, pair_i, pair_j, pair_count, block_fill, block_body):
    length, width = block_fill.shape
    count = (length + 2) * (width + 2)
    framed = jax.ShapeDtypeStruct((length + 2, width + 2, 8, 128), F32)
    eight = [pltpu.SemaphoreType.DMA((8,))] * 2
    ahead = [pltpu.VMEM((9, 128, 128), F32)] * 2
    table = pl.pallas_call(
        lambda *refs: pack_kernel(length, width, *refs),
        out_shape=framed,
        in_specs=[VMEM, VMEM, SMEM],
        out_specs=VMEM,
        scratch_shapes=eight,
        compiler_params=remote(0),
        name="pack",
    )(positions, velocities, block_fill)
    features, density, pressed = pl.pallas_call(
        lambda *refs: density_kernel(length, width, *refs),
        out_shape=(
            jax.ShapeDtypeStruct((count, 128, FEAT), BF16),
            jax.ShapeDtypeStruct((length, width, 128), F32),
            jax.ShapeDtypeStruct((length, width, 8, 128), F32),
        ),
        in_specs=[VMEM],
        out_specs=(VMEM,) * 3,
        scratch_shapes=ahead,
        compiler_params=PARAMS,
        name="density",
    )(table.reshape(count, 8, 128))
    table = pl.pallas_call(
        lambda *refs: frame_kernel(length, width, *refs),
        out_shape=framed,
        in_specs=[VMEM],
        out_specs=VMEM,
        scratch_shapes=eight,
        compiler_params=remote(1),
        name="frame",
    )(pressed)
    accel, partial_force = pl.pallas_call(
        lambda *refs: force_kernel(length, width, *refs),
        out_shape=(
            jax.ShapeDtypeStruct((3, length, width, 128), F32),
            jax.ShapeDtypeStruct((NBODY + 1, 8, 128), F32),
        ),
        in_specs=[SMEM] + [VMEM] * 2,
        out_specs=(VMEM, VMEM),
        scratch_shapes=[pltpu.VMEM((count, 32, 256), BF16)] + ahead,
        compiler_params=PARAMS,
        name="force",
    )(block_body, table.reshape(count, 8, 128), features)
    slabs = lax.axis_size("slab")
    acrosses = lax.axis_size("cross") * lax.axis_size("sub")
    one = partial_force.shape
    totals = pl.pallas_call(
        total_kernel,
        out_shape=jax.ShapeDtypeStruct(one, F32),
        in_specs=[VMEM],
        out_specs=VMEM,
        scratch_shapes=[
            pltpu.VMEM(one, F32),
            pltpu.VMEM((acrosses - 1,) + one, F32),
            pltpu.VMEM((slabs - 1,) + one, F32),
        ]
        + [pltpu.SemaphoreType.DMA((acrosses + slabs - 2,))] * 2,
        compiler_params=remote(2),
        name="total",
    )(partial_force)
    slot_total = 128 * length * slabs * width * acrosses
    body_force = totals[:NBODY, :3, 0].T / math.sqrt(slot_total)
    return (density, accel, body_force)


def solution(mesh):
    placed = (
        P(None, ("tank", "slab"), ("cross", "sub"), None),
        P(None, ("tank", "slab"), ("cross", "sub"), None),
        P(("tank", "slab"), ("cross", "sub"), None),
        P(("tank", "slab"), ("cross", "sub"), None),
        P(("tank", "slab"), ("cross", "sub")),
        P(("tank", "slab"), ("cross", "sub")),
        P(("tank", "slab"), ("cross", "sub")),
    )
    return jax.shard_map(
        shards,
        mesh=mesh,
        in_specs=placed,
        out_specs=(
            P(("tank", "slab"), ("cross", "sub"), None),
            P(None, ("tank", "slab"), ("cross", "sub"), None),
            P(None, "tank"),
        ),
        check_vma=False,
    )
```
